32 devices in a mesh: grp: 4 (over y, core), dev: 8 (over z, x).
Axes of the slice: x: 2, y: 2, z: 4, core: 2. Of those that a mesh axis runs over, the one named last changes fastest.
Arguments:
- queries: bfloat16 [3072, 1024], P('dev'), may hold values from -16 to 16
- docs: bfloat16 [4096, 1024], P(('grp', 'dev')), may hold values from -16 to 16
- compat: int32 [24, 32], P('dev', 'grp'), may hold values from 0 to 1, as said below
- positives: int32 [3072], P('dev'), may hold values from 0 to 4095, as said below
Outputs:
- loss: float32 [3072], P('dev')
- query_grad: float32 [3072, 1024], P('dev')
- doc_grad: float32 [4096, 1024], P(('grp', 'dev'))
The draws below stay inside these ranges and needn't reach their ends.
Inputs may be any that keep to these rules, and one draw needn't show every extreme that they name: compat[b, b % 32] is 1 for every query block b. positives[i] lies in a document block that is compatible with the block of query i.
All inputs are finite; a program needn't handle non-finite values.
Results may differ from the reference program's by a relative error of at most 0.0007.
Values may be sent and summed in bfloat16 or wider, within the bound.
A program may use at most 128 MiB of HBM per device.

```python
import math
import jax
import jax.numpy as jnp
from jax import lax

D = 1024
BLOCK = 128
NQ = 3072
ND = 4096


STRENGTHS = (1.3, 1.8, 2.3)


LOGIT_SCALE = 0.1


ANCHOR_ENERGY = 1000.0


def row_scales(key, rows):
    return jnp.exp(jax.random.uniform(key, (rows, 1), jnp.float32, math.log(0.7), math.log(0.95)))


def base_values(key, rows):
    return jnp.clip(jax.random.normal(key, (rows, D), jnp.float32), -3.5, 3.5)


def anchor_rows(key):
    blocks = ND // BLOCK
    half = (jnp.arange(D) < D // 2).astype(jnp.float32)[None, :]
    magnitude = jnp.sqrt(2.0 * ANCHOR_ENERGY / D)
    signs = 2.0 * jax.random.randint(jax.random.fold_in(key, 31), (blocks, D), 0, 2).astype(jnp.float32) - 1.0
    anchor = magnitude * signs * half
    other = jnp.clip(jax.random.normal(jax.random.fold_in(key, 32), (blocks, D), jnp.float32), -3.5, 3.5) * (1.0 - half)
    ratio = 1.0 - 2.0 / (LOGIT_SCALE * 1.8 * ANCHOR_ENERGY)
    return (anchor, ratio * anchor + other)


def draw_docs(key, part):
    table = row_scales(jax.random.fold_in(key, 11), ND) * base_values(jax.random.fold_in(key, 12), ND)
    anchor, partner = anchor_rows(key)
    blocks = table.reshape(ND // BLOCK, BLOCK, D)
    blocks = blocks.at[:, 0].set(anchor).at[:, 1].set(partner)
    table = blocks.reshape(ND, D)
    return table.astype(jnp.bfloat16)


def draw_queries(key, part):
    table = row_scales(jax.random.fold_in(key, 41), NQ) * base_values(jax.random.fold_in(key, 42), NQ)
    anchor, partner = anchor_rows(key)
    qblocks = NQ // BLOCK
    picks = jnp.arange(qblocks) % (ND // BLOCK)
    strength = jnp.array(STRENGTHS, jnp.float32)[jnp.arange(qblocks) % 3]
    aligned = strength[:, None] * anchor[picks]
    table = table.reshape(qblocks, BLOCK, D).at[:, 0].set(aligned).reshape(NQ, D)
    return table.astype(jnp.bfloat16)


def compat_table(key):
    qblocks = NQ // BLOCK
    dblocks = ND // BLOCK
    limits = jax.random.randint(jax.random.fold_in(key, 21), (qblocks, 1), 80, 700)
    bits = jax.random.randint(jax.random.fold_in(key, 22), (qblocks, dblocks), 0, 1000)
    table = (bits < limits).astype(jnp.int32)
    home = (jnp.arange(dblocks)[None, :] == (jnp.arange(qblocks) % dblocks)[:, None]).astype(jnp.int32)
    return jnp.maximum(table, home)


def draw_compat(key, part):
    return compat_table(key)


def draw_positives(key, part):
    dblocks = ND // BLOCK
    table = compat_table(key)
    ranks = jax.random.randint(jax.random.fold_in(key, 23), (NQ, dblocks), 0, 1048576) * dblocks + jnp.arange(dblocks, dtype=jnp.int32)[None, :]
    allowed = table[jnp.arange(NQ) // BLOCK]
    ranks = jnp.where(allowed > 0, ranks, -1)
    best = lax.top_k(ranks, 1)[1][:, 0].astype(jnp.int32)
    offset = jax.random.randint(jax.random.fold_in(key, 24), (NQ,), 0, BLOCK)
    return (best * BLOCK + offset).astype(jnp.int32)


def setup_inputs(seed: int = 0) -> dict:
    streams_of = jax.random.split(jax.random.key(seed), 5)
    return {
        "queries": draw_queries(jax.random.fold_in(streams_of[4], 71), 0),
        "docs": draw_docs(jax.random.fold_in(streams_of[4], 71), 0),
        "compat": draw_compat(jax.random.fold_in(streams_of[4], 71), 0),
        "positives": draw_positives(jax.random.fold_in(streams_of[4], 71), 0),
    }


LOGIT_SCALE = 0.1
NEG_FLOOR = -1.0e30


def reference(queries, docs, compat, positives):
    count = NQ // BLOCK
    doc_ids = jnp.arange(ND, dtype=jnp.int32)
    query_blocks = queries.reshape(count, BLOCK, D)
    positive_blocks = positives.reshape(count, BLOCK)

    def one_block(doc_total, pieces):
        rows, allowed, wanted = pieces
        scores = LOGIT_SCALE * lax.dot_general(rows, docs, (((1,), (1,)), ((), ())), preferred_element_type=jnp.float32)
        live = jnp.repeat(allowed, BLOCK)[None, :] > 0
        target = doc_ids[None, :] == wanted[:, None]
        row_max = jnp.max(jnp.where(live, scores, NEG_FLOOR), axis=1)
        total = jnp.sum(jnp.where(live, jnp.exp(scores - row_max[:, None]), 0.0), axis=1)
        lse = row_max + jnp.log(total)
        chosen = jnp.sum(jnp.where(target, scores, 0.0), axis=1)
        prob = jnp.where(live, jnp.exp(scores - lse[:, None]), 0.0)
        coef = (prob - target.astype(jnp.float32)).astype(jnp.bfloat16)
        query_part = LOGIT_SCALE * jnp.dot(coef, docs, preferred_element_type=jnp.float32)
        doc_total = doc_total + LOGIT_SCALE * lax.dot_general(coef, rows, (((0,), (0,)), ((), ())), preferred_element_type=jnp.float32)
        return doc_total, (lse - chosen, query_part)

    doc_grad, (loss, query_grad) = lax.scan(one_block, jnp.zeros((ND, D), jnp.float32), (query_blocks, compat, positive_blocks))
    return loss.reshape(NQ), query_grad.reshape(NQ, D), doc_grad
```

```python
import functools
import jax
import jax.numpy as jnp
from jax import lax
from jax.experimental import pallas as pl
from jax.experimental.pallas import tpu as pltpu
from jax.sharding import PartitionSpec as P

BLOCK = 128
LOGIT_SCALE = 0.1
NEG_FLOOR = -1e30
CHUNK = 256
MESH = pl.DeviceIdType.MESH


def nt_dot(a, b):
    return lax.dot_general(a, b, (((1,), (1,)), ((), ())), preferred_element_type=jnp.float32)


def kernel(A, B, C, q_ref, docs_ref, compat_ref, pos_ref,
           loss_ref, qg_ref, dg_ref,
           docs_all, q_all, scores, coef_t, coef, run, st_all, packs,
           q_part, k1_recv, y_all, dd, dd_recv,
           du_s, du_r, dn_s, dn_r, dx_s, dx_r,
           qu_s, qu_r, qd_s, qd_r, qy_s, qy_r, qk_s, qk_r,
           st_s, st_r, pk_s, pk_r,
           k1_s, k1_r, gy_s, gy_r, k2_s, k2_r, dd_s, dd_r):
    n = A * B
    G = 2 * C
    rows, width = q_ref.shape
    panel = docs_ref.shape[0]
    qblocks = rows // BLOCK
    per = panel // BLOCK
    quarter = rows // G
    chunks = width // CHUNK
    half = chunks // 2
    me = lax.axis_index("dev")
    g = lax.axis_index("grp")
    a, b = me // B, me % B
    c, k = g // 2, g % 2

    def push(src, dst, ss, rs, grp, dev):
        pltpu.make_async_remote_copy(
            src_ref=src, dst_ref=dst, send_sem=ss, recv_sem=rs,
            device_id=(grp, dev), device_id_type=MESH).start()

    def sent(like, ss, rs):
        pltpu.make_async_remote_copy(
            src_ref=like, dst_ref=like, send_sem=ss, recv_sem=rs,
            device_id=(g, me), device_id_type=MESH).wait_send()

    def arrive(dst, ss, rs):
        pltpu.make_async_remote_copy(
            src_ref=dst, dst_ref=dst, send_sem=ss, recv_sem=rs,
            device_id=(g, me), device_id_type=MESH).wait_recv()

    barrier = pltpu.get_barrier_semaphore()
    friends = [(g, lax.rem(a + r, A) * B + b) for r in range(1, A)]
    friends += [(g, a * B + lax.rem(b + r, B)) for r in range(1, B)]
    friends += [(lax.rem(g + r, G), me) for r in range(1, G)]
    for f in friends:
        pl.semaphore_signal(barrier, inc=1, device_id=f, device_id_type=MESH)
    pl.semaphore_wait(barrier, len(friends))

    up_ok, dn_ok = a + 1 < A, a >= 1

    def dslot(owner_row, col):
        return docs_all.at[pl.ds((owner_row * B + col) * panel, panel)]

    def docs_up(s, src):
        @pl.when(up_ok)
        def _():
            push(src, dslot(a - s, b), du_s.at[s], du_r.at[s], g, me + B)

    def docs_dn(s, src):
        @pl.when(dn_ok)
        def _():
            push(src, dslot(a + s, b), dn_s.at[s], dn_r.at[s], g, me - B)

    def docs_x(owner, src):
        for r in range(1, B):
            i = owner * (B - 1) + r - 1
            push(src, dslot(owner, b), dx_s.at[i], dx_r.at[i], g,
                 a * B + lax.rem(b + r, B))

    def docs_x_arrive(owner):
        for r in range(1, B):
            i = owner * (B - 1) + r - 1
            arrive(dslot(owner, lax.rem(b + B - r, B)), dx_s.at[i], dx_r.at[i])

    docs_up(0, docs_ref)
    docs_dn(0, docs_ref)
    docs_x(a, docs_ref)
    docs_all[pl.ds(me * panel, panel), :] = docs_ref[...]

    lane_block = lax.broadcasted_iota(jnp.int32, (1, rows), 1) // BLOCK
    own = packs.at[a]
    own[1:2, :] = pos_ref[...].astype(jnp.float32)
    for j in range(n * per):
        line = jnp.zeros((1, rows), jnp.int32)
        for i in range(qblocks):
            line = jnp.where(lane_block == i, compat_ref[i, j], line)
        own[2 + j:3 + j, :] = line.astype(jnp.float32)
    run[0:1, :] = jnp.full((1, rows), NEG_FLOOR, jnp.float32)
    run[1:2, :] = jnp.zeros((1, rows), jnp.float32)

    sub = lax.broadcasted_iota(jnp.int32, (BLOCK, rows), 0)

    def masks(pack, j):
        live = pack[pl.ds(2 + j, 1), :] > 0.0
        ids = (sub + (g * n * per + j) * BLOCK).astype(jnp.float32)
        return live, ids == pack[1:2, :]

    def score_row(owner):
        def one(t, carry):
            j = owner * B * per + t
            at = pl.ds(j * BLOCK, BLOCK)
            s = LOGIT_SCALE * nt_dot(docs_all[at, :], q_ref[...])
            scores[at, :] = s
            live, target = masks(own, j)
            top = jnp.max(jnp.where(live, s, NEG_FLOOR), axis=0, keepdims=True)
            run[0:1, :] = jnp.maximum(run[0:1, :], top)
            run[1:2, :] += jnp.sum(jnp.where(target, s, 0.0), axis=0, keepdims=True)
            return carry
        lax.fori_loop(0, B * per, one, 0)

    my_rows = pl.ds(g * quarter, quarter)

    def q_up(s, src):
        push(src, q_all.at[a - s, my_rows], qu_s.at[s], qu_r.at[s], g, me + B)

    def q_dn(s, src):
        push(src, q_all.at[a + s, my_rows], qd_s.at[s], qd_r.at[s], g, me - B)

    def q_start():
        @pl.when(up_ok)
        def _():
            q_up(0, q_ref.at[my_rows])

        @pl.when(dn_ok)
        def _():
            q_dn(0, q_ref.at[my_rows])

    def valid(s):
        return (a - 1 - s >= 0, a - 1 - s), (a + 1 + s < A, a + 1 + s)

    for s in range(A - 1):
        (uv, uo), (dv, do) = valid(s)

        @pl.when(uv)
        def _():
            arrive(dslot(uo, b), du_s.at[s], du_r.at[s])
            if s < A - 2:
                docs_up(s + 1, dslot(uo, b))
            docs_x(uo, dslot(uo, b))

        @pl.when(dv)
        def _():
            arrive(dslot(do, b), dn_s.at[s], dn_r.at[s])
            if s < A - 2:
                docs_dn(s + 1, dslot(do, b))
            docs_x(do, dslot(do, b))

        if s == max(A - 3, 0):
            q_start()
        if s == 0:
            docs_x_arrive(a)
            score_row(a)
        else:
            for ok, owner in valid(s - 1):
                @pl.when(ok)
                def _():
                    docs_x_arrive(owner)
                    score_row(owner)
    for ok, owner in valid(A - 2):
        @pl.when(ok)
        def _():
            docs_x_arrive(owner)
            score_row(owner)

    def q_relay(s):
        (uv, uo), (dv, do) = valid(s)

        def spread(owner):
            piece = q_all.at[owner, my_rows]
            for r in range(1, C):
                i = owner * (C - 1) + r - 1
                push(piece, piece, qy_s.at[i], qy_r.at[i],
                     lax.rem(c + r, C) * 2 + k, me)
            i = owner * C + c
            push(piece, piece, qk_s.at[i], qk_r.at[i], c * 2 + 1 - k, me)

        @pl.when(uv)
        def _():
            arrive(q_all.at[uo, my_rows], qu_s.at[s], qu_r.at[s])
            if s < A - 2:
                @pl.when(up_ok)
                def _():
                    q_up(s + 1, q_all.at[uo, my_rows])
            spread(uo)

        @pl.when(dv)
        def _():
            arrive(q_all.at[do, my_rows], qd_s.at[s], qd_r.at[s])
            if s < A - 2:
                @pl.when(dn_ok)
                def _():
                    q_dn(s + 1, q_all.at[do, my_rows])
            spread(do)

    def q_cross(s):
        for ok, owner in valid(s):
            @pl.when(ok)
            def _():
                for r in range(1, C):
                    i = owner * (C - 1) + r - 1
                    cc = lax.rem(c + C - r, C)
                    piece = q_all.at[owner, pl.ds((cc * 2 + k) * quarter, quarter)]
                    arrive(piece, qy_s.at[i], qy_r.at[i])
                    i = owner * C + cc
                    push(piece, piece, qk_s.at[i], qk_r.at[i], c * 2 + 1 - k, me)

    def q_arrive(owner):
        for cc in range(C):
            i = owner * C + cc
            piece = q_all.at[owner, pl.ds((cc * 2 + 1 - k) * quarter, quarter)]
            arrive(piece, qk_s.at[i], qk_r.at[i])

    top = run[0:1, :]

    def add_total(j, total):
        live, _ = masks(own, j)
        s = scores[pl.ds(j * BLOCK, BLOCK), :]
        terms = jnp.where(live, jnp.exp(s - top), 0.0)
        return total + jnp.sum(terms, axis=0, keepdims=True)

    total = lax.fori_loop(0, n * per, add_total, jnp.zeros((1, rows), jnp.float32))
    mine = st_all.at[g]
    mine[0:1, :] = top
    mine[1:2, :] = total
    mine[2:3, :] = run[1:2, :]
    for r in range(1, G):
        push(mine, mine, st_s.at[r - 1], st_r.at[r - 1], lax.rem(g + r, G), me)
    q_relay(0)
    for r in range(1, G):
        arrive(st_all.at[lax.rem(g + G - r, G)], st_s.at[r - 1], st_r.at[r - 1])
    top = st_all[0, 0:1, :]
    for i in range(1, G):
        top = jnp.maximum(top, st_all[i, 0:1, :])
    total = jnp.zeros((1, rows), jnp.float32)
    chosen = jnp.zeros((1, rows), jnp.float32)
    for i in range(G):
        total = total + st_all[i, 1:2, :] * jnp.exp(st_all[i, 0:1, :] - top)
        chosen = chosen + st_all[i, 2:3, :]
    lse = top + jnp.log(total)
    loss_ref[...] = lse - chosen
    own[0:1, :] = lse
    for r in range(1, A):
        push(own, own, pk_s.at[r - 1], pk_r.at[r - 1], g, lax.rem(a + r, A) * B + b)
    q_cross(0)

    def coef_block(j, carry):
        live, target = masks(own, j)
        at = pl.ds(j * BLOCK, BLOCK)
        prob = jnp.where(live, jnp.exp(scores[at, :] - lse), 0.0)
        coef_t[at, :] = (prob - target.astype(jnp.float32)).astype(jnp.bfloat16)
        return carry

    lax.fori_loop(0, n * per, coef_block, 0)
    coef[...] = coef_t[...].T
    if A > 2:
        q_relay(1)

    def grad_chunk(j):
        cols = pl.ds(pl.multiple_of(j * CHUNK, CHUNK), CHUNK)
        return LOGIT_SCALE * jnp.dot(coef[...], docs_all[:, cols],
                                     preferred_element_type=jnp.float32)

    other = c * 2 + 1 - k
    for t in range(half):
        q_part[t] = grad_chunk((1 - k) * half + t)
        push(q_part.at[t], k1_recv.at[t], k1_s.at[t], k1_r.at[t], other, me)
    if A > 2:
        q_cross(1)
    for t in range(half):
        part = grad_chunk(k * half + t)
        arrive(k1_recv.at[t], k1_s.at[t], k1_r.at[t])
        y_all[t, c] = part + k1_recv[t]
        for r in range(1, C):
            i = t * (C - 1) + r - 1
            push(y_all.at[t, c], y_all.at[t, c], gy_s.at[i], gy_r.at[i],
                 lax.rem(c + r, C) * 2 + k, me)
    for s in range(2, A - 1):
        q_relay(s)
        q_cross(s)

    def grad_docs(pack, queries, first):
        def one(t, carry):
            j = a * B * per + t
            at = pl.ds(j * BLOCK, BLOCK)
            s = LOGIT_SCALE * nt_dot(docs_all[at, :], queries[...])
            live, target = masks(pack, j)
            prob = jnp.where(live, jnp.exp(s - pack[0:1, :]), 0.0)
            cf = (prob - target.astype(jnp.float32)).astype(jnp.bfloat16)
            add = LOGIT_SCALE * jnp.dot(cf, queries[...], preferred_element_type=jnp.float32)
            to = pl.ds(t * BLOCK, BLOCK)
            dd[to, :] = add if first else dd[to, :] + add
            return carry
        lax.fori_loop(0, B * per, one, 0)

    grad_docs(own, q_ref, True)

    def remote_docs(s):
        (uv, uo), (dv, do) = valid(s)
        for ok, owner, i in ((uv, uo, s), (dv, do, A - 2 - s)):
            @pl.when(ok)
            def _():
                arrive(packs.at[owner], pk_s.at[i], pk_r.at[i])
                q_arrive(owner)
                grad_docs(packs.at[owner], q_all.at[owner], False)

    def finish_chunk(t):
        for r in range(1, C):
            i = t * (C - 1) + r - 1
            arrive(y_all.at[t, lax.rem(c + C - r, C)], gy_s.at[i], gy_r.at[i])
        value = y_all[t, 0]
        for i in range(1, C):
            value = value + y_all[t, i]
        cols = pl.ds(pl.multiple_of((k * half + t) * CHUNK, CHUNK), CHUNK)
        qg_ref[:, cols] = value
        push(qg_ref.at[:, cols], qg_ref.at[:, cols], k2_s.at[t], k2_r.at[t], other, me)

    for s in range(A - 1):
        remote_docs(s)
    for r in range(1, B):
        peer = lax.rem(b + r, B)
        push(dd.at[pl.ds(peer * panel, panel)], dd_recv.at[r - 1], dd_s.at[r - 1],
             dd_r.at[r - 1], g, a * B + peer)
    for t in range(half):
        finish_chunk(t)
    value = dd[pl.ds(b * panel, panel), :]
    for r in range(1, B):
        arrive(dd_recv.at[r - 1], dd_s.at[r - 1], dd_r.at[r - 1])
        value = value + dd_recv[r - 1]
    dg_ref[...] = value
    for t in range(half):
        cols = pl.ds(pl.multiple_of(((1 - k) * half + t) * CHUNK, CHUNK), CHUNK)
        arrive(qg_ref.at[:, cols], k2_s.at[t], k2_r.at[t])

    piece = q_ref.at[pl.ds(0, quarter)]
    for s in range(A - 1):
        @pl.when(jnp.logical_and(up_ok, a - s >= 0))
        def _():
            sent(docs_ref, du_s.at[s], du_r.at[s])
            sent(piece, qu_s.at[s], qu_r.at[s])

        @pl.when(jnp.logical_and(dn_ok, a + s < A))
        def _():
            sent(docs_ref, dn_s.at[s], dn_r.at[s])
            sent(piece, qd_s.at[s], qd_r.at[s])

        sent(own, pk_s.at[s], pk_r.at[s])
    for i in range(A * (B - 1)):
        sent(docs_ref, dx_s.at[i], dx_r.at[i])
    for owner in range(A):
        @pl.when(owner != a)
        def _():
            for i in range(owner * (C - 1), (owner + 1) * (C - 1)):
                sent(piece, qy_s.at[i], qy_r.at[i])
            for i in range(owner * C, (owner + 1) * C):
                sent(piece, qk_s.at[i], qk_r.at[i])
    for r in range(G - 1):
        sent(mine, st_s.at[r], st_r.at[r])
    for t in range(half):
        sent(q_part.at[t], k1_s.at[t], k1_r.at[t])
        cols = pl.ds(pl.multiple_of((k * half + t) * CHUNK, CHUNK), CHUNK)
        sent(qg_ref.at[:, cols], k2_s.at[t], k2_r.at[t])
        for i in range(t * (C - 1), (t + 1) * (C - 1)):
            sent(y_all.at[t, c], gy_s.at[i], gy_r.at[i])
    for r in range(B - 1):
        sent(dd_recv.at[r], dd_s.at[r], dd_r.at[r])


def local(grp, dev, queries, docs, compat, positives):
    A = 4 if dev % 4 == 0 else dev
    B = dev // A
    C = grp // 2
    rows, width = queries.shape
    panel = docs.shape[0]
    n = A * B
    half = width // CHUNK // 2
    pack_rows = -(-(2 + n * panel // BLOCK) // 8) * 8
    f32, bf16 = jnp.float32, jnp.bfloat16
    dma = pltpu.SemaphoreType.DMA
    sems = []
    for count in (A - 1, A - 1, A * (B - 1), A - 1, A - 1, A * (C - 1), A * C,
                  grp - 1, A - 1, half, half * (C - 1), half, B - 1):
        sems += [dma((max(count, 1),))] * 2
    vmem = pl.BlockSpec(memory_space=pltpu.VMEM)
    loss, query_grad, doc_grad = pl.pallas_call(
        functools.partial(kernel, A, B, C),
        out_shape=(
            jax.ShapeDtypeStruct((1, rows), f32),
            jax.ShapeDtypeStruct((rows, width), f32),
            jax.ShapeDtypeStruct((panel, width), f32),
        ),
        in_specs=[vmem, vmem, pl.BlockSpec(memory_space=pltpu.SMEM), vmem],
        out_specs=(vmem, vmem, vmem),
        scratch_shapes=[
            pltpu.VMEM((n * panel, width), bf16),
            pltpu.VMEM((A, rows, width), bf16),
            pltpu.VMEM((n * panel, rows), f32),
            pltpu.VMEM((n * panel, rows), bf16),
            pltpu.VMEM((rows, n * panel), bf16),
            pltpu.VMEM((8, rows), f32),
            pltpu.VMEM((grp, 8, rows), f32),
            pltpu.VMEM((A, pack_rows, rows), f32),
            pltpu.VMEM((half, rows, CHUNK), f32),
            pltpu.VMEM((half, rows, CHUNK), f32),
            pltpu.VMEM((half, C, rows, CHUNK), f32),
            pltpu.VMEM((B * panel, width), f32),
            pltpu.VMEM((max(B - 1, 1), panel, width), f32),
        ] + sems,
        compiler_params=pltpu.CompilerParams(
            collective_id=0, has_side_effects=True, vmem_limit_bytes=56 * 1024 * 1024),
    )(queries, docs, compat, positives.reshape(1, rows))
    return loss.reshape(rows), query_grad, doc_grad


def solution(mesh):
    return jax.shard_map(
        functools.partial(local, mesh.shape["grp"], mesh.shape["dev"]),
        mesh=mesh,
        in_specs=(P("dev", None), P(("grp", "dev"), None), P("dev", "grp"), P("dev")),
        out_specs=(P("dev"), P("dev", None), P(("grp", "dev"), None)),
        check_vma=False,
    )
```

```python
import functools
import jax
import jax.numpy as jnp
from jax import lax
from jax.experimental import pallas as pl
from jax.experimental.pallas import tpu as pltpu
from jax.sharding import PartitionSpec as P

BLOCK = 128
LOGIT_SCALE = 0.1
NEG_FLOOR = -1e30
CHUNK = 256
MESH = pl.DeviceIdType.MESH


def nt_dot(a, b):
    return lax.dot_general(a, b, (((1,), (1,)), ((), ())), preferred_element_type=jnp.float32)


def kernel(A, B, C, PD, PQ, q_ref, docs_ref, compat_ref, pos_ref,
           loss_ref, qg_ref, dg_ref,
           docs_all, q_all, scores, coef_t, coef, run, st_all, packs,
           q_part, k1_recv, y_all, dd, dd_recv,
           du_s, du_r, dn_s, dn_r, dx_s, dx_r,
           qu_s, qu_r, qd_s, qd_r, qy_s, qy_r, qk_s, qk_r,
           st_s, st_r, pk_s, pk_r,
           k1_s, k1_r, gy_s, gy_r, k2_s, k2_r, dd_s, dd_r):
    n = A * B
    G = 2 * C
    rows, width = q_ref.shape
    panel = docs_ref.shape[0]
    qblocks = rows // BLOCK
    per = panel // BLOCK
    quarter = rows // G
    ph, qp = panel // PD, quarter // PQ
    chunks = width // CHUNK
    half = chunks // 2
    me = lax.axis_index("dev")
    g = lax.axis_index("grp")
    a, b = me // B, me % B
    c, k = g // 2, g % 2

    def push(src, dst, ss, rs, grp, dev):
        pltpu.make_async_remote_copy(
            src_ref=src, dst_ref=dst, send_sem=ss, recv_sem=rs,
            device_id=(grp, dev), device_id_type=MESH).start()

    def sent(like, ss, rs):
        pltpu.make_async_remote_copy(
            src_ref=like, dst_ref=like, send_sem=ss, recv_sem=rs,
            device_id=(g, me), device_id_type=MESH).wait_send()

    def arrive(dst, ss, rs):
        pltpu.make_async_remote_copy(
            src_ref=dst, dst_ref=dst, send_sem=ss, recv_sem=rs,
            device_id=(g, me), device_id_type=MESH).wait_recv()

    barrier = pltpu.get_barrier_semaphore()
    friends = [(g, lax.rem(a + r, A) * B + b) for r in range(1, A)]
    friends += [(g, a * B + lax.rem(b + r, B)) for r in range(1, B)]
    friends += [(lax.rem(g + r, G), me) for r in range(1, G)]
    for f in friends:
        pl.semaphore_signal(barrier, inc=1, device_id=f, device_id_type=MESH)
    pl.semaphore_wait(barrier, len(friends))

    up_ok, dn_ok = a + 1 < A, a >= 1

    def dslot(owner_row, col, p):
        return docs_all.at[pl.ds((owner_row * B + col) * panel + p * ph, ph)]

    def docs_up(s, p, src):
        @pl.when(up_ok)
        def _():
            i = s * PD + p
            push(src, dslot(a - s, b, p), du_s.at[i], du_r.at[i], g, me + B)

    def docs_dn(s, p, src):
        @pl.when(dn_ok)
        def _():
            i = s * PD + p
            push(src, dslot(a + s, b, p), dn_s.at[i], dn_r.at[i], g, me - B)

    def docs_x(owner, p, src):
        for r in range(1, B):
            i = (owner * (B - 1) + r - 1) * PD + p
            push(src, dslot(owner, b, p), dx_s.at[i], dx_r.at[i], g,
                 a * B + lax.rem(b + r, B))

    def docs_x_arrive(owner):
        for r in range(1, B):
            for p in range(PD):
                i = (owner * (B - 1) + r - 1) * PD + p
                arrive(dslot(owner, lax.rem(b + B - r, B), p), dx_s.at[i], dx_r.at[i])

    for p in range(PD):
        piece = docs_ref.at[pl.ds(p * ph, ph)]
        docs_up(0, p, piece)
        docs_dn(0, p, piece)
        docs_x(a, p, piece)
    docs_all[pl.ds(me * panel, panel), :] = docs_ref[...]

    lane_block = lax.broadcasted_iota(jnp.int32, (1, rows), 1) // BLOCK
    own = packs.at[a]
    own[1:2, :] = pos_ref[...].reshape(1, rows).astype(jnp.float32)
    for j in range(n * per):
        line = jnp.zeros((1, rows), jnp.int32)
        for i in range(qblocks):
            line = jnp.where(lane_block == i, compat_ref[i, j], line)
        own[2 + j:3 + j, :] = line.astype(jnp.float32)
    run[0:1, :] = jnp.full((1, rows), NEG_FLOOR, jnp.float32)
    run[1:2, :] = jnp.zeros((1, rows), jnp.float32)

    sub = lax.broadcasted_iota(jnp.int32, (BLOCK, rows), 0)

    def masks(pack, j):
        live = pack[pl.ds(2 + j, 1), :] > 0.0
        ids = (sub + (g * n * per + j) * BLOCK).astype(jnp.float32)
        return live, ids == pack[1:2, :]

    def score_row(owner):
        def one(t, carry):
            j = owner * B * per + t
            at = pl.ds(j * BLOCK, BLOCK)
            s = LOGIT_SCALE * nt_dot(docs_all[at, :], q_ref[...])
            scores[at, :] = s
            live, target = masks(own, j)
            top = jnp.max(jnp.where(live, s, NEG_FLOOR), axis=0, keepdims=True)
            run[0:1, :] = jnp.maximum(run[0:1, :], top)
            run[1:2, :] += jnp.sum(jnp.where(target, s, 0.0), axis=0, keepdims=True)
            return carry
        lax.fori_loop(0, B * per, one, 0)

    def share(member, p):
        return pl.ds(member * quarter + p * qp, qp)

    def q_up(s, p, src):
        i = s * PQ + p
        push(src, q_all.at[a - s, share(g, p)], qu_s.at[i], qu_r.at[i], g, me + B)

    def q_dn(s, p, src):
        i = s * PQ + p
        push(src, q_all.at[a + s, share(g, p)], qd_s.at[i], qd_r.at[i], g, me - B)

    def q_start():
        for p in range(PQ):
            @pl.when(up_ok)
            def _():
                q_up(0, p, q_ref.at[share(g, p)])

            @pl.when(dn_ok)
            def _():
                q_dn(0, p, q_ref.at[share(g, p)])

    def valid(s):
        return (a - 1 - s >= 0, a - 1 - s), (a + 1 + s < A, a + 1 + s)

    for s in range(A - 1):
        (uv, uo), (dv, do) = valid(s)

        for p in range(PD):
            @pl.when(uv)
            def _():
                i = s * PD + p
                arrive(dslot(uo, b, p), du_s.at[i], du_r.at[i])
                if s < A - 2:
                    docs_up(s + 1, p, dslot(uo, b, p))
                docs_x(uo, p, dslot(uo, b, p))

            @pl.when(dv)
            def _():
                i = s * PD + p
                arrive(dslot(do, b, p), dn_s.at[i], dn_r.at[i])
                if s < A - 2:
                    docs_dn(s + 1, p, dslot(do, b, p))
                docs_x(do, p, dslot(do, b, p))

        if s == max(A - 3, 0):
            q_start()
        if s == 0:
            docs_x_arrive(a)
            score_row(a)
        else:
            for ok, owner in valid(s - 1):
                @pl.when(ok)
                def _():
                    docs_x_arrive(owner)
                    score_row(owner)
    def q_relay(s):
        (uv, uo), (dv, do) = valid(s)

        def spread(owner, p):
            piece = q_all.at[owner, share(g, p)]
            for r in range(1, C):
                i = (owner * (C - 1) + r - 1) * PQ + p
                push(piece, piece, qy_s.at[i], qy_r.at[i],
                     lax.rem(c + r, C) * 2 + k, me)
            i = (owner * C + c) * PQ + p
            push(piece, piece, qk_s.at[i], qk_r.at[i], c * 2 + 1 - k, me)

        for p in range(PQ):
            i = s * PQ + p

            @pl.when(uv)
            def _():
                piece = q_all.at[uo, share(g, p)]
                arrive(piece, qu_s.at[i], qu_r.at[i])
                if s < A - 2:
                    @pl.when(up_ok)
                    def _():
                        q_up(s + 1, p, piece)
                spread(uo, p)

            @pl.when(dv)
            def _():
                piece = q_all.at[do, share(g, p)]
                arrive(piece, qd_s.at[i], qd_r.at[i])
                if s < A - 2:
                    @pl.when(dn_ok)
                    def _():
                        q_dn(s + 1, p, piece)
                spread(do, p)

    def q_cross(s):
        for p in range(PQ):
            for ok, owner in valid(s):
                @pl.when(ok)
                def _():
                    for r in range(1, C):
                        i = (owner * (C - 1) + r - 1) * PQ + p
                        cc = lax.rem(c + C - r, C)
                        piece = q_all.at[owner, share(cc * 2 + k, p)]
                        arrive(piece, qy_s.at[i], qy_r.at[i])
                        i = (owner * C + cc) * PQ + p
                        push(piece, piece, qk_s.at[i], qk_r.at[i], c * 2 + 1 - k, me)

    def q_arrive(owner):
        for p in range(PQ):
            for cc in range(C):
                i = (owner * C + cc) * PQ + p
                piece = q_all.at[owner, share(cc * 2 + 1 - k, p)]
                arrive(piece, qk_s.at[i], qk_r.at[i])

    q_relay(0)
    for ok, owner in valid(A - 2):
        @pl.when(ok)
        def _():
            docs_x_arrive(owner)
            score_row(owner)

    top = run[0:1, :]

    def add_total(j, total):
        live, _ = masks(own, j)
        s = scores[pl.ds(j * BLOCK, BLOCK), :]
        terms = jnp.where(live, jnp.exp(s - top), 0.0)
        return total + jnp.sum(terms, axis=0, keepdims=True)

    total = lax.fori_loop(0, n * per, add_total, jnp.zeros((1, rows), jnp.float32))
    mine = st_all.at[g]
    mine[0:1, :] = top
    mine[1:2, :] = total
    mine[2:3, :] = run[1:2, :]
    for r in range(1, G):
        push(mine, mine, st_s.at[r - 1], st_r.at[r - 1], lax.rem(g + r, G), me)
    if A > 2:
        q_relay(1)
    for r in range(1, G):
        arrive(st_all.at[lax.rem(g + G - r, G)], st_s.at[r - 1], st_r.at[r - 1])
    top = st_all[0, 0:1, :]
    for i in range(1, G):
        top = jnp.maximum(top, st_all[i, 0:1, :])
    total = jnp.zeros((1, rows), jnp.float32)
    chosen = jnp.zeros((1, rows), jnp.float32)
    for i in range(G):
        total = total + st_all[i, 1:2, :] * jnp.exp(st_all[i, 0:1, :] - top)
        chosen = chosen + st_all[i, 2:3, :]
    lse = top + jnp.log(total)
    loss_ref[...] = (lse - chosen).reshape(rows)
    own[0:1, :] = lse
    for r in range(1, A):
        push(own, own, pk_s.at[r - 1], pk_r.at[r - 1], g, lax.rem(a + r, A) * B + b)
    q_cross(0)

    def coef_block(j, carry):
        live, target = masks(own, j)
        at = pl.ds(j * BLOCK, BLOCK)
        prob = jnp.where(live, jnp.exp(scores[at, :] - lse), 0.0)
        coef_t[at, :] = (prob - target.astype(jnp.float32)).astype(jnp.bfloat16)
        return carry

    lax.fori_loop(0, n * per, coef_block, 0)
    coef[...] = coef_t[...].T

    def grad_chunk(j):
        cols = pl.ds(pl.multiple_of(j * CHUNK, CHUNK), CHUNK)
        return LOGIT_SCALE * jnp.dot(coef[...], docs_all[:, cols],
                                     preferred_element_type=jnp.float32)

    other = c * 2 + 1 - k
    for t in range(half):
        q_part[t] = grad_chunk((1 - k) * half + t)
        push(q_part.at[t], k1_recv.at[t], k1_s.at[t], k1_r.at[t], other, me)
    for t in range(half):
        part = grad_chunk(k * half + t)
        arrive(k1_recv.at[t], k1_s.at[t], k1_r.at[t])
        y_all[t, c] = part + k1_recv[t]
        for r in range(1, C):
            i = t * (C - 1) + r - 1
            push(y_all.at[t, c], y_all.at[t, c], gy_s.at[i], gy_r.at[i],
                 lax.rem(c + r, C) * 2 + k, me)
    for s in range(2, A - 1):
        q_relay(s)
    for s in range(1, A - 1):
        q_cross(s)

    def grad_docs(pack, queries, first):
        def one(t, carry):
            j = a * B * per + t
            at = pl.ds(j * BLOCK, BLOCK)
            s = LOGIT_SCALE * nt_dot(docs_all[at, :], queries[...])
            live, target = masks(pack, j)
            prob = jnp.where(live, jnp.exp(s - pack[0:1, :]), 0.0)
            cf = (prob - target.astype(jnp.float32)).astype(jnp.bfloat16)
            add = LOGIT_SCALE * jnp.dot(cf, queries[...], preferred_element_type=jnp.float32)
            to = pl.ds(t * BLOCK, BLOCK)
            dd[to, :] = add if first else dd[to, :] + add
            return carry
        lax.fori_loop(0, B * per, one, 0)

    grad_docs(own, q_ref, True)

    def remote_docs(s):
        (uv, uo), (dv, do) = valid(s)
        for ok, owner, i in ((uv, uo, s), (dv, do, A - 2 - s)):
            @pl.when(ok)
            def _():
                arrive(packs.at[owner], pk_s.at[i], pk_r.at[i])
                q_arrive(owner)
                grad_docs(packs.at[owner], q_all.at[owner], False)

    def finish_chunk(t):
        for r in range(1, C):
            i = t * (C - 1) + r - 1
            arrive(y_all.at[t, lax.rem(c + C - r, C)], gy_s.at[i], gy_r.at[i])
        value = y_all[t, 0]
        for i in range(1, C):
            value = value + y_all[t, i]
        cols = pl.ds(pl.multiple_of((k * half + t) * CHUNK, CHUNK), CHUNK)
        qg_ref[:, cols] = value
        push(qg_ref.at[:, cols], qg_ref.at[:, cols], k2_s.at[t], k2_r.at[t], other, me)

    for s in range(A - 1):
        remote_docs(s)
    for r in range(1, B):
        peer = lax.rem(b + r, B)
        push(dd.at[pl.ds(peer * panel, panel)], dd_recv.at[r - 1], dd_s.at[r - 1],
             dd_r.at[r - 1], g, a * B + peer)
    for t in range(half):
        finish_chunk(t)
    value = dd[pl.ds(b * panel, panel), :]
    for r in range(1, B):
        arrive(dd_recv.at[r - 1], dd_s.at[r - 1], dd_r.at[r - 1])
        value = value + dd_recv[r - 1]
    dg_ref[...] = value
    for t in range(half):
        cols = pl.ds(pl.multiple_of(((1 - k) * half + t) * CHUNK, CHUNK), CHUNK)
        arrive(qg_ref.at[:, cols], k2_s.at[t], k2_r.at[t])

    qpiece = q_ref.at[pl.ds(0, qp)]
    dpiece = docs_ref.at[pl.ds(0, ph)]
    for s in range(A - 1):
        @pl.when(jnp.logical_and(up_ok, a - s >= 0))
        def _():
            for i in range(s * PD, (s + 1) * PD):
                sent(dpiece, du_s.at[i], du_r.at[i])
            for i in range(s * PQ, (s + 1) * PQ):
                sent(qpiece, qu_s.at[i], qu_r.at[i])

        @pl.when(jnp.logical_and(dn_ok, a + s < A))
        def _():
            for i in range(s * PD, (s + 1) * PD):
                sent(dpiece, dn_s.at[i], dn_r.at[i])
            for i in range(s * PQ, (s + 1) * PQ):
                sent(qpiece, qd_s.at[i], qd_r.at[i])

        sent(own, pk_s.at[s], pk_r.at[s])
    for i in range(A * (B - 1) * PD):
        sent(dpiece, dx_s.at[i], dx_r.at[i])
    for owner in range(A):
        @pl.when(owner != a)
        def _():
            for i in range(owner * (C - 1) * PQ, (owner + 1) * (C - 1) * PQ):
                sent(qpiece, qy_s.at[i], qy_r.at[i])
            for i in range(owner * C * PQ, (owner + 1) * C * PQ):
                sent(qpiece, qk_s.at[i], qk_r.at[i])
    for r in range(G - 1):
        sent(mine, st_s.at[r], st_r.at[r])
    for t in range(half):
        sent(q_part.at[t], k1_s.at[t], k1_r.at[t])
        cols = pl.ds(pl.multiple_of((k * half + t) * CHUNK, CHUNK), CHUNK)
        sent(qg_ref.at[:, cols], k2_s.at[t], k2_r.at[t])
        for i in range(t * (C - 1), (t + 1) * (C - 1)):
            sent(y_all.at[t, c], gy_s.at[i], gy_r.at[i])
    for r in range(B - 1):
        sent(dd_recv.at[r], dd_s.at[r], dd_r.at[r])


def local(grp, dev, queries, docs, compat, positives):
    A = 4 if dev % 4 == 0 else dev
    B = dev // A
    C = grp // 2
    PD = 2
    PQ = 2 if queries.shape[0] // grp % 32 == 0 else 1
    rows, width = queries.shape
    panel = docs.shape[0]
    n = A * B
    half = width // CHUNK // 2
    pack_rows = -(-(2 + n * panel // BLOCK) // 8) * 8
    f32, bf16 = jnp.float32, jnp.bfloat16
    dma = pltpu.SemaphoreType.DMA
    sems = []
    for count in ((A - 1) * PD, (A - 1) * PD, A * (B - 1) * PD,
                  (A - 1) * PQ, (A - 1) * PQ, A * (C - 1) * PQ, A * C * PQ,
                  grp - 1, A - 1, half, half * (C - 1), half, B - 1):
        sems += [dma((max(count, 1),))] * 2
    vmem = pl.BlockSpec(memory_space=pltpu.VMEM)
    loss, query_grad, doc_grad = pl.pallas_call(
        functools.partial(kernel, A, B, C, PD, PQ),
        out_shape=(
            jax.ShapeDtypeStruct((rows,), f32),
            jax.ShapeDtypeStruct((rows, width), f32),
            jax.ShapeDtypeStruct((panel, width), f32),
        ),
        in_specs=[vmem, vmem, pl.BlockSpec(memory_space=pltpu.SMEM), vmem],
        out_specs=(vmem, vmem, vmem),
        scratch_shapes=[
            pltpu.VMEM((n * panel, width), bf16),
            pltpu.VMEM((A, rows, width), bf16),
            pltpu.VMEM((n * panel, rows), f32),
            pltpu.VMEM((n * panel, rows), bf16),
            pltpu.VMEM((rows, n * panel), bf16),
            pltpu.VMEM((8, rows), f32),
            pltpu.VMEM((grp, 8, rows), f32),
            pltpu.VMEM((A, pack_rows, rows), f32),
            pltpu.VMEM((half, rows, CHUNK), f32),
            pltpu.VMEM((half, rows, CHUNK), f32),
            pltpu.VMEM((half, C, rows, CHUNK), f32),
            pltpu.VMEM((B * panel, width), f32),
            pltpu.VMEM((max(B - 1, 1), panel, width), f32),
        ] + sems,
        compiler_params=pltpu.CompilerParams(
            collective_id=0, has_side_effects=True, vmem_limit_bytes=56 * 1024 * 1024),
    )(queries, docs, compat, positives)
    return loss, query_grad, doc_grad


def solution(mesh):
    return jax.shard_map(
        functools.partial(local, mesh.shape["grp"], mesh.shape["dev"]),
        mesh=mesh,
        in_specs=(P("dev", None), P(("grp", "dev"), None), P("dev", "grp"), P("dev")),
        out_specs=(P("dev"), P("dev", None), P(("grp", "dev"), None)),
        check_vma=False,
    )
```

```python
import functools
import jax
import jax.numpy as jnp
from jax import lax
from jax.experimental import pallas as pl
from jax.experimental.pallas import tpu as pltpu
from jax.sharding import PartitionSpec as P

BLOCK = 128
LOGIT_SCALE = 0.1
NEG_FLOOR = -1e30
CHUNK = 256
MESH = pl.DeviceIdType.MESH


def nt_dot(a, b):
    return lax.dot_general(a, b, (((1,), (1,)), ((), ())), preferred_element_type=jnp.float32)


def kernel(A, B, C, PD, PQ, q_ref, docs_ref, compat_ref, pos_ref,
           loss_ref, qg_ref, dg_ref,
           docs_all, q_all, scores, coef_t, coef, run, st_all, packs,
           q_part, k1_recv, y_all, dd, dd_recv,
           du_s, du_r, dn_s, dn_r, dx_s, dx_r,
           qu_s, qu_r, qd_s, qd_r, qy_s, qy_r, qk_s, qk_r,
           st_s, st_r, pk_s, pk_r,
           k1_s, k1_r, gy_s, gy_r, k2_s, k2_r, dd_s, dd_r):
    n = A * B
    G = 2 * C
    rows, width = q_ref.shape
    panel = docs_ref.shape[0]
    qblocks = rows // BLOCK
    per = panel // BLOCK
    quarter = rows // G
    ph, qp = panel // PD, quarter // PQ
    chunks = width // CHUNK
    half = chunks // 2
    me = lax.axis_index("dev")
    g = lax.axis_index("grp")
    a, b = me // B, me % B
    c, k = g // 2, g % 2

    def push(src, dst, ss, rs, grp, dev):
        pltpu.make_async_remote_copy(
            src_ref=src, dst_ref=dst, send_sem=ss, recv_sem=rs,
            device_id=(grp, dev), device_id_type=MESH).start()

    def sent(like, ss, rs):
        pltpu.make_async_remote_copy(
            src_ref=like, dst_ref=like, send_sem=ss, recv_sem=rs,
            device_id=(g, me), device_id_type=MESH).wait_send()

    def arrive(dst, ss, rs):
        pltpu.make_async_remote_copy(
            src_ref=dst, dst_ref=dst, send_sem=ss, recv_sem=rs,
            device_id=(g, me), device_id_type=MESH).wait_recv()

    barrier = pltpu.get_barrier_semaphore()
    friends = [(g, lax.rem(a + r, A) * B + b) for r in range(1, A)]
    friends += [(g, a * B + lax.rem(b + r, B)) for r in range(1, B)]
    friends += [(lax.rem(g + r, G), me) for r in range(1, G)]
    for f in friends:
        pl.semaphore_signal(barrier, inc=1, device_id=f, device_id_type=MESH)
    pl.semaphore_wait(barrier, len(friends))

    up_ok, dn_ok = a + 1 < A, a >= 1

    def dslot(owner_row, col, p):
        return docs_all.at[pl.ds((owner_row * B + col) * panel + p * ph, ph)]

    def docs_up(s, p, src):
        @pl.when(up_ok)
        def _():
            i = s * PD + p
            push(src, dslot(a - s, b, p), du_s.at[i], du_r.at[i], g, me + B)

    def docs_dn(s, p, src):
        @pl.when(dn_ok)
        def _():
            i = s * PD + p
            push(src, dslot(a + s, b, p), dn_s.at[i], dn_r.at[i], g, me - B)

    def docs_x(owner, p, src):
        for r in range(1, B):
            i = (owner * (B - 1) + r - 1) * PD + p
            push(src, dslot(owner, b, p), dx_s.at[i], dx_r.at[i], g,
                 a * B + lax.rem(b + r, B))

    def docs_x_arrive(owner):
        for r in range(1, B):
            for p in range(PD):
                i = (owner * (B - 1) + r - 1) * PD + p
                arrive(dslot(owner, lax.rem(b + B - r, B), p), dx_s.at[i], dx_r.at[i])

    for p in range(PD):
        piece = docs_ref.at[pl.ds(p * ph, ph)]
        docs_up(0, p, piece)
        docs_dn(0, p, piece)
        docs_x(a, p, piece)
    docs_all[pl.ds(me * panel, panel), :] = docs_ref[...]

    lane_block = lax.broadcasted_iota(jnp.int32, (1, rows), 1) // BLOCK
    own = packs.at[a]
    own[1:2, :] = pos_ref[...].reshape(1, rows).astype(jnp.float32)
    for j in range(n * per):
        line = jnp.zeros((1, rows), jnp.int32)
        for i in range(qblocks):
            line = jnp.where(lane_block == i, compat_ref[i, j], line)
        own[2 + j:3 + j, :] = line.astype(jnp.float32)
    run[0:1, :] = jnp.full((1, rows), NEG_FLOOR, jnp.float32)
    run[1:2, :] = jnp.zeros((1, rows), jnp.float32)

    PAIR = 2 if B * per % 2 == 0 else 1
    span = PAIR * BLOCK
    sub = lax.broadcasted_iota(jnp.int32, (span, rows), 0)

    def masks(pack, j):
        line = pack[pl.ds(2 + j, 1), :]
        if PAIR == 2:
            line = jnp.where(sub < BLOCK, line, pack[pl.ds(3 + j, 1), :])
        ids = (sub + (g * n * per + j) * BLOCK).astype(jnp.float32)
        return line > 0.0, ids == pack[1:2, :]

    def score_row(owner):
        def one(t, carry):
            j = owner * B * per + t * PAIR
            at = pl.ds(j * BLOCK, span)
            s = LOGIT_SCALE * nt_dot(docs_all[at, :], q_ref[...])
            scores[at, :] = s
            live, target = masks(own, j)
            top = jnp.max(jnp.where(live, s, NEG_FLOOR), axis=0, keepdims=True)
            run[0:1, :] = jnp.maximum(run[0:1, :], top)
            run[1:2, :] += jnp.sum(jnp.where(target, s, 0.0), axis=0, keepdims=True)
            return carry
        lax.fori_loop(0, B * per // PAIR, one, 0)

    def share(member, p):
        return pl.ds(member * quarter + p * qp, qp)

    def q_up(s, p, src):
        i = s * PQ + p
        push(src, q_all.at[a - s, share(g, p)], qu_s.at[i], qu_r.at[i], g, me + B)

    def q_dn(s, p, src):
        i = s * PQ + p
        push(src, q_all.at[a + s, share(g, p)], qd_s.at[i], qd_r.at[i], g, me - B)

    def q_start():
        for p in range(PQ):
            @pl.when(up_ok)
            def _():
                q_up(0, p, q_ref.at[share(g, p)])

            @pl.when(dn_ok)
            def _():
                q_dn(0, p, q_ref.at[share(g, p)])

    def valid(s):
        return (a - 1 - s >= 0, a - 1 - s), (a + 1 + s < A, a + 1 + s)

    def q_relay(s):
        (uv, uo), (dv, do) = valid(s)

        def spread(owner, p):
            piece = q_all.at[owner, share(g, p)]
            for r in range(1, C):
                i = (owner * (C - 1) + r - 1) * PQ + p
                push(piece, piece, qy_s.at[i], qy_r.at[i],
                     lax.rem(c + r, C) * 2 + k, me)
            i = (owner * C + c) * PQ + p
            push(piece, piece, qk_s.at[i], qk_r.at[i], c * 2 + 1 - k, me)

        for p in range(PQ):
            i = s * PQ + p

            @pl.when(uv)
            def _():
                piece = q_all.at[uo, share(g, p)]
                arrive(piece, qu_s.at[i], qu_r.at[i])
                if s < A - 2:
                    @pl.when(up_ok)
                    def _():
                        q_up(s + 1, p, piece)
                spread(uo, p)

            @pl.when(dv)
            def _():
                piece = q_all.at[do, share(g, p)]
                arrive(piece, qd_s.at[i], qd_r.at[i])
                if s < A - 2:
                    @pl.when(dn_ok)
                    def _():
                        q_dn(s + 1, p, piece)
                spread(do, p)

    def q_cross(s):
        for p in range(PQ):
            for ok, owner in valid(s):
                @pl.when(ok)
                def _():
                    for r in range(1, C):
                        i = (owner * (C - 1) + r - 1) * PQ + p
                        cc = lax.rem(c + C - r, C)
                        piece = q_all.at[owner, share(cc * 2 + k, p)]
                        arrive(piece, qy_s.at[i], qy_r.at[i])
                        i = (owner * C + cc) * PQ + p
                        push(piece, piece, qk_s.at[i], qk_r.at[i], c * 2 + 1 - k, me)

    def q_arrive(owner):
        for p in range(PQ):
            for cc in range(C):
                i = (owner * C + cc) * PQ + p
                piece = q_all.at[owner, share(cc * 2 + 1 - k, p)]
                arrive(piece, qk_s.at[i], qk_r.at[i])

    LAG = 2

    def relay_at(point):
        if 0 <= point - LAG < A - 1:
            q_relay(point - LAG)

    for s in range(A - 1):
        (uv, uo), (dv, do) = valid(s)

        for p in range(PD):
            @pl.when(uv)
            def _():
                i = s * PD + p
                arrive(dslot(uo, b, p), du_s.at[i], du_r.at[i])
                if s < A - 2:
                    docs_up(s + 1, p, dslot(uo, b, p))
                docs_x(uo, p, dslot(uo, b, p))

            @pl.when(dv)
            def _():
                i = s * PD + p
                arrive(dslot(do, b, p), dn_s.at[i], dn_r.at[i])
                if s < A - 2:
                    docs_dn(s + 1, p, dslot(do, b, p))
                docs_x(do, p, dslot(do, b, p))

        if s == max(A - 3, 0):
            q_start()
        relay_at(s)
        if s == 0:
            docs_x_arrive(a)
            score_row(a)
        else:
            for ok, owner in valid(s - 1):
                @pl.when(ok)
                def _():
                    docs_x_arrive(owner)
                    score_row(owner)
    for ok, owner in valid(A - 2):
        @pl.when(ok)
        def _():
            docs_x_arrive(owner)
            score_row(owner)

    top = run[0:1, :]

    def add_total(t, total):
        live, _ = masks(own, t * PAIR)
        s = scores[pl.ds(t * span, span), :]
        terms = jnp.where(live, jnp.exp(s - top), 0.0)
        return total + jnp.sum(terms, axis=0, keepdims=True)

    total = lax.fori_loop(0, n * per // PAIR, add_total, jnp.zeros((1, rows), jnp.float32))
    mine = st_all.at[g]
    mine[0:1, :] = top
    mine[1:2, :] = total
    mine[2:3, :] = run[1:2, :]
    for r in range(1, G):
        push(mine, mine, st_s.at[r - 1], st_r.at[r - 1], lax.rem(g + r, G), me)
    relay_at(A - 1)
    for r in range(1, G):
        arrive(st_all.at[lax.rem(g + G - r, G)], st_s.at[r - 1], st_r.at[r - 1])
    top = st_all[0, 0:1, :]
    for i in range(1, G):
        top = jnp.maximum(top, st_all[i, 0:1, :])
    total = jnp.zeros((1, rows), jnp.float32)
    chosen = jnp.zeros((1, rows), jnp.float32)
    for i in range(G):
        total = total + st_all[i, 1:2, :] * jnp.exp(st_all[i, 0:1, :] - top)
        chosen = chosen + st_all[i, 2:3, :]
    lse = top + jnp.log(total)
    loss_ref[...] = (lse - chosen).reshape(rows)
    own[0:1, :] = lse
    for r in range(1, A):
        push(own, own, pk_s.at[r - 1], pk_r.at[r - 1], g, lax.rem(a + r, A) * B + b)
    q_cross(0)

    def coef_block(t, carry):
        live, target = masks(own, t * PAIR)
        at = pl.ds(t * span, span)
        prob = jnp.where(live, jnp.exp(scores[at, :] - lse), 0.0)
        coef_t[at, :] = (prob - target.astype(jnp.float32)).astype(jnp.bfloat16)
        return carry

    lax.fori_loop(0, n * per // PAIR, coef_block, 0)
    coef[...] = coef_t[...].T

    def grad_chunk(j):
        cols = pl.ds(pl.multiple_of(j * CHUNK, CHUNK), CHUNK)
        return LOGIT_SCALE * jnp.dot(coef[...], docs_all[:, cols],
                                     preferred_element_type=jnp.float32)

    other = c * 2 + 1 - k
    for t in range(half):
        q_part[t] = grad_chunk((1 - k) * half + t)
        push(q_part.at[t], k1_recv.at[t], k1_s.at[t], k1_r.at[t], other, me)
    relay_at(A)
    for t in range(half):
        part = grad_chunk(k * half + t)
        arrive(k1_recv.at[t], k1_s.at[t], k1_r.at[t])
        y_all[t, c] = part + k1_recv[t]
        for r in range(1, C):
            i = t * (C - 1) + r - 1
            push(y_all.at[t, c], y_all.at[t, c], gy_s.at[i], gy_r.at[i],
                 lax.rem(c + r, C) * 2 + k, me)
    for s in range(1, A - 1):
        q_cross(s)

    def grad_docs(pack, queries, first):
        def one(t, carry):
            j = a * B * per + t * PAIR
            at = pl.ds(j * BLOCK, span)
            s = LOGIT_SCALE * nt_dot(docs_all[at, :], queries[...])
            live, target = masks(pack, j)
            prob = jnp.where(live, jnp.exp(s - pack[0:1, :]), 0.0)
            cf = (prob - target.astype(jnp.float32)).astype(jnp.bfloat16)
            add = LOGIT_SCALE * jnp.dot(cf, queries[...], preferred_element_type=jnp.float32)
            to = pl.ds(t * span, span)
            dd[to, :] = add if first else dd[to, :] + add
            return carry
        lax.fori_loop(0, B * per // PAIR, one, 0)

    grad_docs(own, q_ref, True)

    def remote_docs(s):
        (uv, uo), (dv, do) = valid(s)
        for ok, owner, i in ((uv, uo, s), (dv, do, A - 2 - s)):
            @pl.when(ok)
            def _():
                arrive(packs.at[owner], pk_s.at[i], pk_r.at[i])
                q_arrive(owner)
                grad_docs(packs.at[owner], q_all.at[owner], False)

    def finish_chunk(t):
        for r in range(1, C):
            i = t * (C - 1) + r - 1
            arrive(y_all.at[t, lax.rem(c + C - r, C)], gy_s.at[i], gy_r.at[i])
        value = y_all[t, 0]
        for i in range(1, C):
            value = value + y_all[t, i]
        cols = pl.ds(pl.multiple_of((k * half + t) * CHUNK, CHUNK), CHUNK)
        qg_ref[:, cols] = value
        push(qg_ref.at[:, cols], qg_ref.at[:, cols], k2_s.at[t], k2_r.at[t], other, me)

    for s in range(A - 1):
        remote_docs(s)
    for r in range(1, B):
        peer = lax.rem(b + r, B)
        push(dd.at[pl.ds(peer * panel, panel)], dd_recv.at[r - 1], dd_s.at[r - 1],
             dd_r.at[r - 1], g, a * B + peer)
    for t in range(half):
        finish_chunk(t)
    value = dd[pl.ds(b * panel, panel), :]
    for r in range(1, B):
        arrive(dd_recv.at[r - 1], dd_s.at[r - 1], dd_r.at[r - 1])
        value = value + dd_recv[r - 1]
    dg_ref[...] = value
    for t in range(half):
        cols = pl.ds(pl.multiple_of(((1 - k) * half + t) * CHUNK, CHUNK), CHUNK)
        arrive(qg_ref.at[:, cols], k2_s.at[t], k2_r.at[t])

    qpiece = q_ref.at[pl.ds(0, qp)]
    dpiece = docs_ref.at[pl.ds(0, ph)]
    for s in range(A - 1):
        @pl.when(jnp.logical_and(up_ok, a - s >= 0))
        def _():
            for i in range(s * PD, (s + 1) * PD):
                sent(dpiece, du_s.at[i], du_r.at[i])
            for i in range(s * PQ, (s + 1) * PQ):
                sent(qpiece, qu_s.at[i], qu_r.at[i])

        @pl.when(jnp.logical_and(dn_ok, a + s < A))
        def _():
            for i in range(s * PD, (s + 1) * PD):
                sent(dpiece, dn_s.at[i], dn_r.at[i])
            for i in range(s * PQ, (s + 1) * PQ):
                sent(qpiece, qd_s.at[i], qd_r.at[i])

        sent(own, pk_s.at[s], pk_r.at[s])
    for i in range(A * (B - 1) * PD):
        sent(dpiece, dx_s.at[i], dx_r.at[i])
    for owner in range(A):
        @pl.when(owner != a)
        def _():
            for i in range(owner * (C - 1) * PQ, (owner + 1) * (C - 1) * PQ):
                sent(qpiece, qy_s.at[i], qy_r.at[i])
            for i in range(owner * C * PQ, (owner + 1) * C * PQ):
                sent(qpiece, qk_s.at[i], qk_r.at[i])
    for r in range(G - 1):
        sent(mine, st_s.at[r], st_r.at[r])
    for t in range(half):
        sent(q_part.at[t], k1_s.at[t], k1_r.at[t])
        cols = pl.ds(pl.multiple_of((k * half + t) * CHUNK, CHUNK), CHUNK)
        sent(qg_ref.at[:, cols], k2_s.at[t], k2_r.at[t])
        for i in range(t * (C - 1), (t + 1) * (C - 1)):
            sent(y_all.at[t, c], gy_s.at[i], gy_r.at[i])
    for r in range(B - 1):
        sent(dd_recv.at[r], dd_s.at[r], dd_r.at[r])


def local(grp, dev, queries, docs, compat, positives):
    A = 4 if dev % 4 == 0 else dev
    B = dev // A
    C = grp // 2
    PD = 2
    PQ = 2 if queries.shape[0] // grp % 32 == 0 else 1
    rows, width = queries.shape
    panel = docs.shape[0]
    n = A * B
    half = width // CHUNK // 2
    pack_rows = -(-(2 + n * panel // BLOCK) // 8) * 8
    f32, bf16 = jnp.float32, jnp.bfloat16
    dma = pltpu.SemaphoreType.DMA
    sems = []
    for count in ((A - 1) * PD, (A - 1) * PD, A * (B - 1) * PD,
                  (A - 1) * PQ, (A - 1) * PQ, A * (C - 1) * PQ, A * C * PQ,
                  grp - 1, A - 1, half, half * (C - 1), half, B - 1):
        sems += [dma((max(count, 1),))] * 2
    vmem = pl.BlockSpec(memory_space=pltpu.VMEM)
    loss, query_grad, doc_grad = pl.pallas_call(
        functools.partial(kernel, A, B, C, PD, PQ),
        out_shape=(
            jax.ShapeDtypeStruct((rows,), f32),
            jax.ShapeDtypeStruct((rows, width), f32),
            jax.ShapeDtypeStruct((panel, width), f32),
        ),
        in_specs=[vmem, vmem, pl.BlockSpec(memory_space=pltpu.SMEM), vmem],
        out_specs=(vmem, vmem, vmem),
        scratch_shapes=[
            pltpu.VMEM((n * panel, width), bf16),
            pltpu.VMEM((A, rows, width), bf16),
            pltpu.VMEM((n * panel, rows), f32),
            pltpu.VMEM((n * panel, rows), bf16),
            pltpu.VMEM((rows, n * panel), bf16),
            pltpu.VMEM((8, rows), f32),
            pltpu.VMEM((grp, 8, rows), f32),
            pltpu.VMEM((A, pack_rows, rows), f32),
            pltpu.VMEM((half, rows, CHUNK), f32),
            pltpu.VMEM((half, rows, CHUNK), f32),
            pltpu.VMEM((half, C, rows, CHUNK), f32),
            pltpu.VMEM((B * panel, width), f32),
            pltpu.VMEM((max(B - 1, 1), panel, width), f32),
        ] + sems,
        compiler_params=pltpu.CompilerParams(
            collective_id=0, has_side_effects=True, vmem_limit_bytes=56 * 1024 * 1024),
    )(queries, docs, compat, positives)
    return loss, query_grad, doc_grad


def solution(mesh):
    return jax.shard_map(
        functools.partial(local, mesh.shape["grp"], mesh.shape["dev"]),
        mesh=mesh,
        in_specs=(P("dev", None), P(("grp", "dev"), None), P("dev", "grp"), P("dev")),
        out_specs=(P("dev"), P("dev", None), P(("grp", "dev"), None)),
        check_vma=False,
    )
```
